128 devices in a mesh: seq: 8 (over z, y_hi), grp: 16 (over y_lo, x, core).
Axes of the slice: x: 4, y: 4 (y_hi: 2, y_lo: 2; y = y_hi * 2 + y_lo), z: 4, core: 2. Of those that a mesh axis runs over, the one named last changes fastest.
Arguments:
- self_query: bfloat16 [16, 1024, 5120], P('grp', 'seq'), may hold values from -250 to 250
- self_key: bfloat16 [16, 1024, 5120], P('grp', 'seq'), may hold values from -12 to 12
- self_value: bfloat16 [16, 1024, 5120], P('grp', 'seq'), may hold values from -6 to 6
- self_upstream: bfloat16 [16, 1024, 5120], P('grp', 'seq'), may hold values from -6 to 6
- cross_query: bfloat16 [16, 1024, 5120], P('grp', 'seq'), may hold values from -250 to 250
- context_key: bfloat16 [512, 5120], replicated, may hold values from -12 to 12
- context_value: bfloat16 [512, 5120], replicated, may hold values from -6 to 6
- cross_upstream: bfloat16 [16, 1024, 5120], P('grp', 'seq'), may hold values from -6 to 6
Outputs:
- query_grad: bfloat16 [16, 1024, 5120], P('grp', 'seq')
- key_grad: bfloat16 [16, 1024, 5120], P('grp', 'seq')
- value_grad: bfloat16 [16, 1024, 5120], P('grp', 'seq')
- cross_query_grad: bfloat16 [16, 1024, 5120], P('grp', 'seq')
- context_key_grad: float32 [512, 5120], P(None, 'seq')
- context_value_grad: float32 [512, 5120], P(None, 'seq')
The draws below stay inside these ranges and needn't reach their ends.
All inputs are finite; a program needn't handle non-finite values.
Results may differ from the reference program's by a relative error of at most 0.013.
Values may be sent and summed in bfloat16 or wider, within the bound.
A program may use at most 256 MiB of HBM per device.

```python
import jax
import jax.numpy as jnp
from jax import lax

D = 5120
HEADS = 40
HD = 128
CTX = 512
LEN = 1024
SAMPLES = 16


def drawn_pair(key, salt, key_samples, key_count):
    base = jax.random.fold_in(key, salt)
    query_key, keys_key = jax.random.split(base, 2)
    queries = jax.random.truncated_normal(query_key, -6.0, 6.0, (SAMPLES, LEN, HEADS, HD), jnp.float32)
    keyset = jax.random.truncated_normal(keys_key, -6.0, 6.0, (key_samples, key_count, HEADS, HD), jnp.float32)
    return (queries.reshape(SAMPLES, LEN, HEADS * HD), keyset.reshape(key_samples, key_count, HEADS * HD))


def draw_self_query(key, part):
    return drawn_pair(key, 11, SAMPLES, LEN)[0].astype(jnp.bfloat16)


def draw_self_key(key, part):
    return drawn_pair(key, 11, SAMPLES, LEN)[1].astype(jnp.bfloat16)


def draw_cross_query(key, part):
    return drawn_pair(key, 23, 1, CTX)[0].astype(jnp.bfloat16)


def draw_context_key(key, part):
    return drawn_pair(key, 23, 1, CTX)[1][0].astype(jnp.bfloat16)


def raised(values, own_key, source, target, parts, factor):
    owner, partner = [(jnp.arange(values.shape[position]) // (values.shape[position] // parts)).reshape([-1 if axis == position else 1 for axis in range(values.ndim)]) for position in (source, target)]
    chosen = jax.random.permutation(own_key, parts)[partner]
    strong = (owner == chosen) | (owner == (partner + parts // 2) % parts)
    return jnp.where(strong, factor * values, values)


def level_of(rng, shape, cuts, low, top_value):
    def one(axis_at, shards_of):
        draws = jax.random.uniform(jax.random.fold_in(jax.random.fold_in(rng, 6), axis_at), (shards_of,), jnp.float32, low / len(cuts), top_value / len(cuts))
        return jnp.repeat(jnp.exp(draws), shape[axis_at] // shards_of).reshape((-1,) + (1,) * (len(shape) - axis_at - 1))

    loudness = one(*cuts[0])
    for cut in cuts[1:]:
        loudness = loudness * one(*cut)
    return loudness


def noise(own_key, shape, spread, bound, cuts=(), kind=jnp.bfloat16):
    level = level_of(own_key, shape, cuts, -0.22, 0.18) if cuts else 1.0
    values = jax.random.normal(own_key, shape, jnp.float32) * spread * level
    return jnp.minimum(jnp.maximum(values, -bound), bound).astype(kind)


def noise_with(rng, shape, width, limit, cuts, heavy, dtype=jnp.bfloat16):
    result = width * jax.random.normal(rng, shape, jnp.float32)
    if cuts:
        result = result * level_of(rng, shape, cuts, -0.22, 0.18)
    return jnp.clip(raised(result, jax.random.fold_in(rng, 3), *heavy), -limit, limit).astype(dtype)


def setup_inputs(seed: int = 0) -> dict:
    splits = jax.random.split(jax.random.key(seed), 9)
    return {
        "self_query": draw_self_query(jax.random.fold_in(splits[8], 71), 0),
        "self_key": draw_self_key(jax.random.fold_in(splits[8], 71), 0),
        "self_value": noise(splits[2], (SAMPLES, LEN, D), 1.0, 6.0, ((0, 16), (1, 8))),
        "self_upstream": noise(splits[3], (SAMPLES, LEN, D), 1.0, 6.0, ((0, 16), (1, 8))),
        "cross_query": draw_cross_query(jax.random.fold_in(splits[8], 71), 0),
        "context_key": draw_context_key(jax.random.fold_in(splits[8], 71), 0),
        "context_value": noise(splits[6], (CTX, D), 1.0, 6.0),
        "cross_upstream": noise_with(splits[7], (SAMPLES, LEN, D), 1.0, 6.0, ((0, 16), (1, 8)), (1, 2, 8, 2.0)),
    }


def attend_back(queries, key_in, value_in, upstream):
    scaling = HD ** -0.5
    query_f = queries.astype(jnp.float32)
    key_f = key_in.astype(jnp.float32)
    value_f = value_in.astype(jnp.float32)
    upstream_f = upstream.astype(jnp.float32)
    scores = jnp.einsum("nhe,mhe->hnm", query_f, key_f) * scaling
    weights = jax.nn.softmax(scores, axis=-1)
    rounded = lax.optimization_barrier(weights.astype(jnp.bfloat16)).astype(jnp.float32)
    output = jnp.einsum("hnm,mhe->nhe", rounded, value_f)
    row_inner = jnp.sum(upstream_f * output, axis=-1)
    grad_prob = jnp.einsum("nhe,mhe->hnm", upstream_f, value_f)
    grad_score = weights * (grad_prob - jnp.transpose(row_inner)[:, :, None]) * scaling
    grad_score = lax.optimization_barrier(grad_score.astype(jnp.bfloat16)).astype(jnp.float32)
    query_grad = jnp.einsum("hnm,mhe->nhe", grad_score, key_f)
    key_grad = jnp.einsum("hnm,nhe->mhe", grad_score, query_f)
    value_grad = jnp.einsum("hnm,nhe->mhe", rounded, upstream_f)
    return query_grad, key_grad, value_grad


def reference(self_query, self_key, self_value, self_upstream, cross_query, context_key, context_value, cross_upstream):
    layout = (SAMPLES, LEN, HEADS, HD)

    def one_sample(pieces):
        grads = attend_back(pieces[0], pieces[1], pieces[2], pieces[3])
        return (grads[0].astype(jnp.bfloat16).reshape(LEN, D),
                grads[1].astype(jnp.bfloat16).reshape(LEN, D),
                grads[2].astype(jnp.bfloat16).reshape(LEN, D))

    query_grad, key_grad, value_grad = lax.map(
        one_sample,
        (self_query.reshape(layout), self_key.reshape(layout), self_value.reshape(layout), self_upstream.reshape(layout)))
    context_heads = context_key.reshape(CTX, HEADS, HD)
    value_heads = context_value.reshape(CTX, HEADS, HD)

    def cross_step(totals, pieces):
        grads = attend_back(pieces[0], context_heads, value_heads, pieces[1])
        return (totals[0] + grads[1], totals[1] + grads[2]), grads[0].astype(jnp.bfloat16).reshape(LEN, D)

    zero_sum = jnp.zeros((CTX, HEADS, HD), jnp.float32)
    totals, cross_grad = lax.scan(cross_step, (zero_sum, zero_sum),
                                  (cross_query.reshape(layout), cross_upstream.reshape(layout)))
    return (query_grad, key_grad, value_grad, cross_grad,
            totals[0].reshape(CTX, D), totals[1].reshape(CTX, D))
```

```python
import functools
import math

import jax
import jax.numpy as jnp
from jax import lax
from jax.experimental import pallas as pl
from jax.experimental.pallas import tpu as pltpu
from jax.sharding import PartitionSpec as P

HD = 128
SEQ = 8
XC = 8
MESH = pl.DeviceIdType.MESH
SCALE = HD ** (-0.5)
EXP2_SCALE = SCALE * math.log2(math.e)
BLOCK = 256


def contract(left, right, left_dim, right_dim):
    return lax.dot_general(
        left, right, (((left_dim,), (right_dim,)), ((), ())), preferred_element_type=jnp.float32
    )


def attend_block(queries, upstream, keys, values):
    scores = contract(keys, queries, 1, 1)
    top = jnp.max(scores, axis=0, keepdims=True)
    raised = jnp.exp2((scores - top) * EXP2_SCALE)
    weights = raised * (1.0 / jnp.sum(raised, axis=0, keepdims=True))
    rounded = weights.astype(jnp.bfloat16)
    grad_prob = contract(values, upstream, 1, 1)
    delta = jnp.sum(rounded.astype(jnp.float32) * grad_prob, axis=0, keepdims=True)
    grad_score = (weights * (grad_prob - delta)).astype(jnp.bfloat16)
    value_grad = contract(rounded, upstream, 1, 0)
    key_grad = contract(grad_score, queries, 1, 0)
    query_grad = contract(keys, grad_score, 0, 0).T * SCALE
    return query_grad, key_grad, value_grad


def kernel(
    sq, sk, sv, su, cq, ck, cv, cu,
    oq, ok, ov, ocq, ock, ocv,
    self_in, cross_in, ctx, self_out, cross_out, part, pieces, turned, turned_in, other_in, gathered,
    key_acc, value_acc,
    in_send, in_recv, x_send, x_recv, ctx_sem, o_send, o_recv, xo_send, xo_recv,
    p_send, p_recv, t_send, t_recv, y_send, y_recv, g_send, g_recv,
):
    seq = lax.axis_index("seq")
    grp = lax.axis_index("grp")
    lane = lax.rem(grp, XC)
    row = lax.div(grp, XC)
    heads = self_in.shape[0]
    tokens = sq.shape[1]
    rows = self_in.shape[2]
    text = part.shape[2]
    text_piece = pieces.shape[3]

    def seq_peer(d):
        return lax.rem(seq + d, SEQ)

    def lane_peer(d):
        return lax.rem(lane + d, XC)

    def at_seq(p):
        return {"seq": p, "grp": grp}

    def at_lane(p):
        return {"seq": seq, "grp": row * XC + p}

    turn_to = {"seq": lane, "grp": row * XC + seq}
    other_row = {"seq": seq, "grp": (1 - row) * XC + lane}

    def columns(owner, h):
        return pl.ds(pl.multiple_of((owner * heads + h) * HD, HD), HD)

    def token_rows(owner):
        return pl.ds(pl.multiple_of(owner * tokens, tokens), tokens)

    def text_rows(owner):
        return pl.ds(pl.multiple_of(owner * text_piece, text_piece), text_piece)

    def remote(src, dst, send, recv, where):
        pltpu.make_async_remote_copy(
            src_ref=src, dst_ref=dst, send_sem=send, recv_sem=recv, device_id=where, device_id_type=MESH
        ).start()

    def local(src, dst, sem):
        pltpu.make_async_copy(src, dst, sem).start()

    def drain(ref, sem):
        pltpu.make_async_copy(ref, ref, sem).wait()

    def load_ctx(h, carry):
        local(ck.at[:, columns(lane, h)], ctx.at[0, h], ctx_sem)
        local(cv.at[:, columns(lane, h)], ctx.at[1, h], ctx_sem)
        return carry

    lax.fori_loop(0, heads, load_ctx, 0)

    barrier = pltpu.get_barrier_semaphore()

    def greet(d, carry):
        pl.semaphore_signal(barrier, inc=1, device_id=at_seq(seq_peer(d)), device_id_type=MESH)
        pl.semaphore_signal(barrier, inc=1, device_id=at_lane(lane_peer(d)), device_id_type=MESH)
        return carry

    lax.fori_loop(1, SEQ, greet, 0)
    pl.semaphore_signal(barrier, inc=1, device_id=other_row, device_id_type=MESH)

    @pl.when(lane != seq)
    def _():
        pl.semaphore_signal(barrier, inc=1, device_id=turn_to, device_id_type=MESH)
        pl.semaphore_wait(barrier, SEQ + XC)

    @pl.when(lane == seq)
    def _():
        pl.semaphore_wait(barrier, SEQ + XC - 1)

    def send_in(h, carry):
        for a, ref in enumerate((cq, cu)):
            local(ref.at[0, :, columns(lane, h)], cross_in.at[h, a, token_rows(lane)], x_recv.at[h])
        for a, ref in enumerate((sq, sk, sv, su)):
            local(ref.at[0, :, columns(seq, h)], self_in.at[h, a, token_rows(seq)], in_recv.at[h])

        def to_peer(d, inner):
            p = seq_peer(d)
            e = lane_peer(d)
            for a, ref in enumerate((cq, cu)):
                remote(
                    ref.at[0, :, columns(e, h)], cross_in.at[h, a, token_rows(lane)],
                    x_send, x_recv.at[h], at_lane(e),
                )
            for a, ref in enumerate((sq, sk, sv, su)):
                remote(
                    ref.at[0, :, columns(p, h)], self_in.at[h, a, token_rows(seq)],
                    in_send, in_recv.at[h], at_seq(p),
                )
            return inner

        lax.fori_loop(1, SEQ, to_peer, 0)
        return carry

    lax.fori_loop(0, heads, send_in, 0)

    drain(ctx, ctx_sem)

    def cross_head(h, carry):
        drain(cross_in.at[h], x_recv.at[h])
        key_acc[pl.ds(0, text), :] = jnp.zeros((text, HD), jnp.float32)
        value_acc[pl.ds(0, text), :] = jnp.zeros((text, HD), jnp.float32)

        def block(b, inner):
            at = pl.ds(pl.multiple_of(b * BLOCK, BLOCK), BLOCK)
            query_grad, key_grad, value_grad = attend_block(
                cross_in[h, 0, at, :], cross_in[h, 1, at, :], ctx[0, h], ctx[1, h]
            )
            cross_out[h, at, :] = query_grad.astype(jnp.bfloat16)
            key_acc[pl.ds(0, text), :] += key_grad
            value_acc[pl.ds(0, text), :] += value_grad
            return inner

        lax.fori_loop(0, rows // BLOCK, block, 0)
        part[h, 0] = (key_acc[pl.ds(0, text), :] * SCALE).astype(jnp.bfloat16)
        part[h, 1] = value_acc[pl.ds(0, text), :].astype(jnp.bfloat16)

        local(cross_out.at[h, token_rows(lane)], ocq.at[0, :, columns(lane, h)], xo_recv)
        local(part.at[h, :, text_rows(seq)], pieces.at[seq, h], p_recv)

        def to_peer(d, inner):
            p = seq_peer(d)
            e = lane_peer(d)
            remote(
                cross_out.at[h, token_rows(e)], ocq.at[0, :, columns(lane, h)], xo_send, xo_recv, at_lane(e)
            )
            remote(part.at[h, :, text_rows(p)], pieces.at[seq, h], p_send, p_recv, at_seq(p))
            return inner

        lax.fori_loop(1, SEQ, to_peer, 0)
        return carry

    lax.fori_loop(0, heads, cross_head, 0)

    def self_head(h, carry):
        drain(self_in.at[h], in_recv.at[h])
        key_acc[...] = jnp.zeros_like(key_acc)
        value_acc[...] = jnp.zeros_like(value_acc)

        def block(b, inner):
            at = pl.ds(pl.multiple_of(b * BLOCK, BLOCK), BLOCK)
            query_grad, key_grad, value_grad = attend_block(
                self_in[h, 0, at, :], self_in[h, 3, at, :], self_in[h, 1], self_in[h, 2]
            )
            self_out[h, 0, at, :] = query_grad.astype(jnp.bfloat16)
            key_acc[...] += key_grad
            value_acc[...] += value_grad
            return inner

        lax.fori_loop(0, rows // BLOCK, block, 0)
        self_out[h, 1] = (key_acc[...] * SCALE).astype(jnp.bfloat16)
        self_out[h, 2] = value_acc[...].astype(jnp.bfloat16)

        for a, ref in enumerate((oq, ok, ov)):
            local(self_out.at[h, a, token_rows(seq)], ref.at[0, :, columns(seq, h)], o_recv.at[a])

        def to_peer(d, inner):
            p = seq_peer(d)
            for a, ref in enumerate((oq, ok, ov)):
                remote(
                    self_out.at[h, a, token_rows(p)], ref.at[0, :, columns(seq, h)],
                    o_send, o_recv.at[a], at_seq(p),
                )
            return inner

        lax.fori_loop(1, SEQ, to_peer, 0)

        @pl.when(h == 1)
        def _():
            drain(pieces, p_recv)
            total = pieces[0].astype(jnp.float32)
            for i in range(1, SEQ):
                total = total + pieces[i].astype(jnp.float32)
            turned[...] = total

            @pl.when(lane == seq)
            def _():
                local(turned, turned_in, t_recv)

            @pl.when(lane != seq)
            def _():
                remote(turned, turned_in, t_send, t_recv, turn_to)

        @pl.when(h == 2)
        def _():
            drain(turned_in, t_recv)
            remote(turned_in, other_in, y_send, y_recv, other_row)

        @pl.when(h == 3)
        def _():
            drain(other_in, y_recv)
            gathered[lane] = (turned_in[...] + other_in[...]).astype(jnp.bfloat16)

            def to_lane(d, inner):
                remote(gathered.at[lane], gathered.at[lane], g_send, g_recv, at_lane(lane_peer(d)))
                return inner

            lax.fori_loop(1, XC, to_lane, 0)

        return carry

    lax.fori_loop(0, heads, self_head, 0)

    drain(gathered.at[pl.ds(0, XC - 1)], g_recv)
    for h in range(heads):
        for j in range(XC):
            ock[pl.ds(j * text_piece, text_piece), pl.ds(h * HD, HD)] = gathered[j, h, 0].astype(jnp.float32)
            ocv[pl.ds(j * text_piece, text_piece), pl.ds(h * HD, HD)] = gathered[j, h, 1].astype(jnp.float32)

    others = rows - tokens
    drain(self_in.at[:, :, pl.ds(0, others)], in_send)
    drain(cross_in.at[:, :, pl.ds(0, others)], x_send)
    drain(cross_out.at[:, pl.ds(0, others)], xo_send)
    drain(pieces.at[pl.ds(0, SEQ - 1)], p_send)

    @pl.when(lane != seq)
    def _():
        drain(turned, t_send)

    drain(turned_in, y_send)
    drain(gathered.at[pl.ds(0, XC - 1)], g_send)
    drain(self_out.at[:, :, pl.ds(0, others)], o_send)
    drain(ocq, xo_recv)
    for a, ref in enumerate((oq, ok, ov)):
        drain(ref, o_recv.at[a])


def shards(sq, sk, sv, su, cq, ck, cv, cu):
    tokens, width = sq.shape[1], sq.shape[2]
    text = ck.shape[0]
    rows = tokens * SEQ
    heads = width // HD // SEQ
    piece = text // SEQ
    half, full = jnp.bfloat16, jnp.float32
    token_out = jax.ShapeDtypeStruct((1, tokens, width), half)
    text_out = jax.ShapeDtypeStruct((text, width // SEQ), full)
    in_any = pl.BlockSpec(memory_space=pl.ANY)
    in_vmem = pl.BlockSpec(memory_space=pltpu.VMEM)
    dma = pltpu.SemaphoreType.DMA
    return pl.pallas_call(
        kernel,
        out_shape=(token_out,) * 4 + (text_out,) * 2,
        in_specs=[in_any] * 8,
        out_specs=(in_any,) * 4 + (in_vmem,) * 2,
        scratch_shapes=[
            pltpu.VMEM((heads, 4, rows, HD), half),
            pltpu.VMEM((heads, 2, rows, HD), half),
            pltpu.VMEM((2, heads, text, HD), half),
            pltpu.VMEM((heads, 3, rows, HD), half),
            pltpu.VMEM((heads, rows, HD), half),
            pltpu.VMEM((heads, 2, text, HD), half),
            pltpu.VMEM((SEQ, heads, 2, piece, HD), half),
            pltpu.VMEM((heads, 2, piece, HD), full),
            pltpu.VMEM((heads, 2, piece, HD), full),
            pltpu.VMEM((heads, 2, piece, HD), full),
            pltpu.VMEM((XC, heads, 2, piece, HD), half),
            pltpu.VMEM((rows, HD), full),
            pltpu.VMEM((rows, HD), full),
            dma, dma((heads,)), dma, dma((heads,)), dma, dma, dma((3,)), dma, dma,
            dma, dma, dma, dma, dma, dma, dma, dma,
        ],
        compiler_params=pltpu.CompilerParams(
            collective_id=0, has_side_effects=True, vmem_limit_bytes=58 << 20
        ),
        cost_estimate=pl.CostEstimate(flops=10 << 30, bytes_accessed=16 << 20, transcendentals=8 << 20),
    )(sq, sk, sv, su, cq, ck, cv, cu)


def solution(mesh):
    token = P("grp", "seq", None)
    return jax.shard_map(
        shards,
        mesh=mesh,
        in_specs=(token, token, token, token, token, P(), P(), token),
        out_specs=(token, token, token, token, P(None, "seq"), P(None, "seq")),
        check_vma=False,
    )
```

```python
import functools
import math

import jax
import jax.numpy as jnp
from jax import lax
from jax.experimental import pallas as pl
from jax.experimental.pallas import tpu as pltpu
from jax.sharding import PartitionSpec as P

HD = 128
SEQ = 8
XC = 8
MESH = pl.DeviceIdType.MESH
SCALE = HD ** (-0.5)
EXP2_SCALE = SCALE * math.log2(math.e)
BLOCK = 256
EARLY = 3
LATE = 1
STAGES = (1, 2, 3, 4)


def contract(left, right, left_dim, right_dim):
    return lax.dot_general(
        left, right, (((left_dim,), (right_dim,)), ((), ())), preferred_element_type=jnp.float32
    )


def attend_block(queries, upstream, keys, values):
    scores = contract(keys, queries, 1, 1)
    top = jnp.max(scores, axis=0, keepdims=True)
    raised = jnp.exp2((scores - top) * EXP2_SCALE)
    weights = raised * (1.0 / jnp.sum(raised, axis=0, keepdims=True))
    rounded = weights.astype(jnp.bfloat16)
    grad_prob = contract(values, upstream, 1, 1)
    delta = jnp.sum(rounded.astype(jnp.float32) * grad_prob, axis=0, keepdims=True)
    grad_score = (weights * (grad_prob - delta)).astype(jnp.bfloat16)
    value_grad = contract(rounded, upstream, 1, 0)
    key_grad = contract(grad_score, queries, 1, 0)
    query_grad = contract(keys, grad_score, 0, 0).T * SCALE
    return query_grad, key_grad, value_grad


def kernel(
    sq, sk, sv, su, cq, ck, cv, cu,
    oq, ok, ov, ocq, ock, ocv,
    self_in, cross_in, ctx, self_out, cross_out, part, first, mid, second, turned, gathered,
    key_acc, value_acc,
    in_send, in_recv, x_send, x_recv, ctx_sem, o_send, o_recv, xo_send, xo_recv,
    a_send, a_recv, b_send, b_recv, t_send, t_recv, y_send, y_recv, g_send, g_recv,
):
    seq = lax.axis_index("seq")
    grp = lax.axis_index("grp")
    lane = lax.rem(grp, XC)
    row = lax.div(grp, XC)
    along_z = lax.div(seq, 2)
    high = lax.rem(seq, 2)
    along_y = high * 2 + row
    heads = self_in.shape[0]
    tokens = sq.shape[1]
    rows = self_in.shape[2]
    text = part.shape[2]
    quarter = mid.shape[2]
    piece = turned.shape[2]

    def seq_peer(d):
        return lax.rem(seq + d, SEQ)

    def lane_peer(d):
        return lax.rem(lane + d, XC)

    def at_seq(p):
        return {"seq": p, "grp": grp}

    def at_lane(p):
        return {"seq": seq, "grp": row * XC + p}

    def at_y(p):
        return {"seq": along_z * 2 + lax.div(p, 2), "grp": lax.rem(p, 2) * XC + lane}

    def at_z(p):
        return {"seq": p * 2 + high, "grp": grp}

    turn_to = {"seq": lane, "grp": row * XC + seq}
    other_row = {"seq": seq, "grp": (1 - row) * XC + lane}
    other_corner = {"seq": along_z * 2 + 1 - high, "grp": (1 - row) * XC + lane}

    def columns(owner, h):
        return pl.ds(pl.multiple_of((owner * heads + h) * HD, HD), HD)

    def part_rows(owner, size):
        return pl.ds(pl.multiple_of(owner * size, size), size)

    def token_rows(owner):
        return part_rows(owner, tokens)

    def remote(src, dst, send, recv, where):
        pltpu.make_async_remote_copy(
            src_ref=src, dst_ref=dst, send_sem=send, recv_sem=recv, device_id=where, device_id_type=MESH
        ).start()

    def local(src, dst, sem):
        pltpu.make_async_copy(src, dst, sem).start()

    def drain(ref, sem):
        pltpu.make_async_copy(ref, ref, sem).wait()

    def load_ctx(h, carry):
        local(ck.at[:, columns(lane, h)], ctx.at[0, h], ctx_sem)
        local(cv.at[:, columns(lane, h)], ctx.at[1, h], ctx_sem)
        return carry

    lax.fori_loop(0, heads, load_ctx, 0)

    barrier = pltpu.get_barrier_semaphore()

    def greet(d, carry):
        pl.semaphore_signal(barrier, inc=1, device_id=at_seq(seq_peer(d)), device_id_type=MESH)
        pl.semaphore_signal(barrier, inc=1, device_id=at_lane(lane_peer(d)), device_id_type=MESH)
        return carry

    lax.fori_loop(1, SEQ, greet, 0)
    pl.semaphore_signal(barrier, inc=1, device_id=other_row, device_id_type=MESH)
    pl.semaphore_signal(barrier, inc=1, device_id=other_corner, device_id_type=MESH)

    @pl.when(lane != seq)
    def _():
        pl.semaphore_signal(barrier, inc=1, device_id=turn_to, device_id_type=MESH)
        pl.semaphore_wait(barrier, SEQ + XC + 1)

    @pl.when(lane == seq)
    def _():
        pl.semaphore_wait(barrier, SEQ + XC)

    def send_cross(h, carry):
        for a, ref in enumerate((cq, cu)):
            local(ref.at[0, :, columns(lane, h)], cross_in.at[h, a, token_rows(lane)], x_recv.at[h])

        def to_peer(d, inner):
            e = lane_peer(d)
            for a, ref in enumerate((cq, cu)):
                remote(
                    ref.at[0, :, columns(e, h)], cross_in.at[h, a, token_rows(lane)],
                    x_send, x_recv.at[h], at_lane(e),
                )
            return inner

        lax.fori_loop(1, XC, to_peer, 0)
        return carry

    def send_self(h, carry):
        for a, ref in enumerate((sq, sk, sv, su)):
            local(ref.at[0, :, columns(seq, h)], self_in.at[h, a, token_rows(seq)], in_recv.at[h])

        def to_peer(d, inner):
            p = seq_peer(d)
            for a, ref in enumerate((sq, sk, sv, su)):
                remote(
                    ref.at[0, :, columns(p, h)], self_in.at[h, a, token_rows(seq)],
                    in_send, in_recv.at[h], at_seq(p),
                )
            return inner

        lax.fori_loop(1, SEQ, to_peer, 0)
        return carry

    def send_both(h, carry):
        send_cross(h, carry)
        return send_self(h, carry)

    lax.fori_loop(0, EARLY, send_both, 0)
    lax.fori_loop(EARLY, heads, send_cross, 0)

    drain(ctx, ctx_sem)

    def cross_head(h, carry):
        drain(cross_in.at[h], x_recv.at[h])
        key_acc[pl.ds(0, text), :] = jnp.zeros((text, HD), jnp.float32)
        value_acc[pl.ds(0, text), :] = jnp.zeros((text, HD), jnp.float32)

        def block(b, inner):
            at = pl.ds(pl.multiple_of(b * BLOCK, BLOCK), BLOCK)
            query_grad, key_grad, value_grad = attend_block(
                cross_in[h, 0, at, :], cross_in[h, 1, at, :], ctx[0, h], ctx[1, h]
            )
            cross_out[h, at, :] = query_grad.astype(jnp.bfloat16)
            key_acc[pl.ds(0, text), :] += key_grad
            value_acc[pl.ds(0, text), :] += value_grad
            return inner

        lax.fori_loop(0, rows // BLOCK, block, 0)
        part[h, 0] = (key_acc[pl.ds(0, text), :] * SCALE).astype(jnp.bfloat16)
        part[h, 1] = value_acc[pl.ds(0, text), :].astype(jnp.bfloat16)

        local(part.at[h, 0, part_rows(along_y, quarter)], first.at[0, along_y, h], a_recv)
        local(part.at[h, 1, part_rows(along_z, quarter)], first.at[1, along_z, h], a_recv)

        def to_quarter(d, inner):
            p = lax.rem(along_y + d, 4)
            remote(part.at[h, 0, part_rows(p, quarter)], first.at[0, along_y, h], a_send, a_recv, at_y(p))
            p = lax.rem(along_z + d, 4)
            remote(part.at[h, 1, part_rows(p, quarter)], first.at[1, along_z, h], a_send, a_recv, at_z(p))
            return inner

        lax.fori_loop(1, 4, to_quarter, 0)

        local(cross_out.at[h, token_rows(lane)], ocq.at[0, :, columns(lane, h)], xo_recv)

        def to_peer(d, inner):
            e = lane_peer(d)
            remote(
                cross_out.at[h, token_rows(e)], ocq.at[0, :, columns(lane, h)], xo_send, xo_recv, at_lane(e)
            )
            return inner

        lax.fori_loop(1, XC, to_peer, 0)
        return carry

    lax.fori_loop(0, heads, cross_head, 0)

    def sum_quarters():
        drain(first, a_recv)

        def one(h, carry):
            for a in range(2):
                total = first[a, 0, h].astype(jnp.float32)
                for i in range(1, 4):
                    total = total + first[a, i, h].astype(jnp.float32)
                mid[a, h] = total.astype(jnp.bfloat16)
            return carry

        lax.fori_loop(0, heads, one, 0)
        local(mid.at[0, :, part_rows(along_z, piece)], second.at[0, along_z], b_recv)
        local(mid.at[1, :, part_rows(along_y, piece)], second.at[1, along_y], b_recv)

        def to_piece(d, carry):
            p = lax.rem(along_z + d, 4)
            remote(mid.at[0, :, part_rows(p, piece)], second.at[0, along_z], b_send, b_recv, at_z(p))
            p = lax.rem(along_y + d, 4)
            remote(mid.at[1, :, part_rows(p, piece)], second.at[1, along_y], b_send, b_recv, at_y(p))
            return carry

        lax.fori_loop(1, 4, to_piece, 0)

    def sum_pieces():
        drain(second, b_recv)
        for a in range(2):
            total = second[a, 0].astype(jnp.float32)
            for i in range(1, 4):
                total = total + second[a, i].astype(jnp.float32)
            turned[a] = total.astype(jnp.bfloat16)

        @pl.when(lane == seq)
        def _():
            local(turned, gathered.at[lane, row], t_recv)

        @pl.when(lane != seq)
        def _():
            remote(turned, gathered.at[seq, row], t_send, t_recv, turn_to)

    def share_rows():
        drain(turned, t_recv)
        remote(gathered.at[lane, row], gathered.at[lane, row], y_send, y_recv, other_row)

    def share_lanes():
        drain(turned, y_recv)

        def to_lane(d, inner):
            remote(gathered.at[lane], gathered.at[lane], g_send, g_recv, at_lane(lane_peer(d)))
            return inner

        lax.fori_loop(1, XC, to_lane, 0)

    def self_head(h, carry):
        @pl.when(h == 0)
        def _():
            send_self(EARLY, 0)

        for position, step in enumerate((sum_quarters, sum_pieces, share_rows, share_lanes)):
            pl.when(h == STAGES[position])(step)

        @pl.when(h == LATE)
        def _():
            send_self(EARLY + 1, 0)

        drain(self_in.at[h], in_recv.at[h])
        key_acc[...] = jnp.zeros_like(key_acc)
        value_acc[...] = jnp.zeros_like(value_acc)

        def block(b, inner):
            at = pl.ds(pl.multiple_of(b * BLOCK, BLOCK), BLOCK)
            query_grad, key_grad, value_grad = attend_block(
                self_in[h, 0, at, :], self_in[h, 3, at, :], self_in[h, 1], self_in[h, 2]
            )
            self_out[h, 0, at, :] = query_grad.astype(jnp.bfloat16)
            key_acc[...] += key_grad
            value_acc[...] += value_grad
            return inner

        lax.fori_loop(0, rows // BLOCK, block, 0)
        self_out[h, 1] = (key_acc[...] * SCALE).astype(jnp.bfloat16)
        self_out[h, 2] = value_acc[...].astype(jnp.bfloat16)

        for a, ref in enumerate((oq, ok, ov)):
            local(self_out.at[h, a, token_rows(seq)], ref.at[0, :, columns(seq, h)], o_recv.at[a])

        def to_peer(d, inner):
            p = seq_peer(d)
            for a, ref in enumerate((oq, ok, ov)):
                remote(
                    self_out.at[h, a, token_rows(p)], ref.at[0, :, columns(seq, h)],
                    o_send, o_recv.at[a], at_seq(p),
                )
            return inner

        lax.fori_loop(1, SEQ, to_peer, 0)
        return carry

    lax.fori_loop(0, heads, self_head, 0)

    drain(gathered.at[pl.ds(0, XC - 1)], g_recv)
    for h in range(heads):
        at = pl.ds(h * HD, HD)
        for e in range(XC):
            z, y_high = divmod(e, 2)
            for r in range(2):
                y = y_high * 2 + r
                ock[pl.ds(y * quarter + z * piece, piece), at] = gathered[e, r, 0, h].astype(jnp.float32)
                ocv[pl.ds(z * quarter + y * piece, piece), at] = gathered[e, r, 1, h].astype(jnp.float32)

    others = rows - tokens
    drain(self_in.at[:, :, pl.ds(0, others)], in_send)
    drain(cross_in.at[:, :, pl.ds(0, others)], x_send)
    drain(cross_out.at[:, pl.ds(0, others)], xo_send)
    drain(first.at[:, pl.ds(0, 3)], a_send)
    drain(second.at[:, pl.ds(0, 3)], b_send)

    @pl.when(lane != seq)
    def _():
        drain(turned, t_send)

    drain(turned, y_send)
    drain(gathered.at[pl.ds(0, XC - 1)], g_send)
    drain(self_out.at[:, :, pl.ds(0, others)], o_send)
    drain(ocq, xo_recv)
    for a, ref in enumerate((oq, ok, ov)):
        drain(ref, o_recv.at[a])


def to_hbm(*refs):
    count = len(refs) // 2
    sems = refs[-1]
    copies = [pltpu.make_async_copy(refs[i], refs[count + i], sems.at[i]) for i in range(count)]
    for copy in copies:
        copy.start()
    for copy in copies:
        copy.wait()


def shards(sq, sk, sv, su, cq, ck, cv, cu):
    tokens, width = sq.shape[1], sq.shape[2]
    text = ck.shape[0]
    rows = tokens * SEQ
    heads = width // HD // SEQ
    quarter, piece = text // 4, text // 16
    half, full = jnp.bfloat16, jnp.float32
    token_shape = ((1, tokens, width), half)
    text_shape = ((text, width // SEQ), full)
    out_shapes = (token_shape,) * 4 + (text_shape,) * 2
    in_any = pl.BlockSpec(memory_space=pl.ANY)
    in_vmem = pl.BlockSpec(memory_space=pltpu.VMEM)
    dma = pltpu.SemaphoreType.DMA
    results = pl.pallas_call(
        kernel,
        out_shape=tuple(pltpu.VMEM(*shape) for shape in out_shapes),
        in_specs=[in_any] * 8,
        out_specs=(in_vmem,) * 6,
        scratch_shapes=[
            pltpu.VMEM((heads, 4, rows, HD), half),
            pltpu.VMEM((heads, 2, rows, HD), half),
            pltpu.VMEM((2, heads, text, HD), half),
            pltpu.VMEM((heads, 3, rows, HD), half),
            pltpu.VMEM((heads, rows, HD), half),
            pltpu.VMEM((heads, 2, text, HD), half),
            pltpu.VMEM((2, 4, heads, quarter, HD), half),
            pltpu.VMEM((2, heads, quarter, HD), half),
            pltpu.VMEM((2, 4, heads, piece, HD), half),
            pltpu.VMEM((2, heads, piece, HD), half),
            pltpu.VMEM((XC, 2, 2, heads, piece, HD), half),
            pltpu.VMEM((rows, HD), full),
            pltpu.VMEM((rows, HD), full),
            dma, dma((heads,)), dma, dma((heads,)), dma, dma, dma((3,)), dma, dma,
            dma, dma, dma, dma, dma, dma, dma, dma, dma, dma,
        ],
        compiler_params=pltpu.CompilerParams(
            collective_id=0, has_side_effects=True, vmem_limit_bytes=46 << 20
        ),
        cost_estimate=pl.CostEstimate(flops=10 << 30, bytes_accessed=16 << 20, transcendentals=8 << 20),
    )(sq, sk, sv, su, cq, ck, cv, cu)
    return pl.pallas_call(
        to_hbm,
        out_shape=tuple(jax.ShapeDtypeStruct(*shape) for shape in out_shapes),
        in_specs=[in_vmem] * 6,
        out_specs=(in_any,) * 6,
        scratch_shapes=[dma((6,))],
        compiler_params=pltpu.CompilerParams(vmem_limit_bytes=1 << 20),
    )(*results)


def solution(mesh):
    token = P("grp", "seq", None)
    return jax.shard_map(
        shards,
        mesh=mesh,
        in_specs=(token, token, token, token, token, P(), P(), token),
        out_specs=(token, token, token, token, P(None, "seq"), P(None, "seq")),
        check_vma=False,
    )
```

```python
import functools
import math

import jax
import jax.numpy as jnp
from jax import lax
from jax.experimental import pallas as pl
from jax.experimental.pallas import tpu as pltpu
from jax.sharding import PartitionSpec as P

HD = 128
SEQ = 8
XC = 8
MESH = pl.DeviceIdType.MESH
SCALE = HD ** (-0.5)
EXP2_SCALE = SCALE * math.log2(math.e)
BLOCK = 256
CHUNKS = 4
EARLY = 3
LATE = 1
STAGES = (1, 2, 3, 4)


def contract(left, right, left_dim, right_dim):
    return lax.dot_general(
        left, right, (((left_dim,), (right_dim,)), ((), ())), preferred_element_type=jnp.float32
    )


def attend_block(queries, upstream, keys, values):
    scores = contract(keys, queries, 1, 1)
    top = jnp.max(scores, axis=0, keepdims=True)
    raised = jnp.exp2((scores - top) * EXP2_SCALE)
    weights = raised * (1.0 / jnp.sum(raised, axis=0, keepdims=True))
    rounded = weights.astype(jnp.bfloat16)
    grad_prob = contract(values, upstream, 1, 1)
    delta = jnp.sum(rounded.astype(jnp.float32) * grad_prob, axis=0, keepdims=True)
    grad_score = (weights * (grad_prob - delta)).astype(jnp.bfloat16)
    value_grad = contract(rounded, upstream, 1, 0)
    key_grad = contract(grad_score, queries, 1, 0)
    query_grad = contract(keys, grad_score, 0, 0).T * SCALE
    return query_grad, key_grad, value_grad


def kernel(
    sq, sk, sv, su, cq, ck, cv, cu,
    oq, ok, ov, ocq, ock, ocv,
    self_in, cross_in, ctx, self_out, cross_out, part, first, mid, second, turned, gathered,
    key_acc, value_acc,
    in_send, in_recv, x_send, x_recv, ctx_sem, o_send, o_recv, xo_send, xo_recv,
    a_send, a_recv, b_send, b_recv, t_send, t_recv, y_send, y_recv, g_send, g_recv,
):
    seq = lax.axis_index("seq")
    grp = lax.axis_index("grp")
    lane = lax.rem(grp, XC)
    row = lax.div(grp, XC)
    along_z = lax.div(seq, 2)
    high = lax.rem(seq, 2)
    along_y = high * 2 + row
    heads = self_in.shape[0]
    tokens = sq.shape[1]
    rows = self_in.shape[2]
    text = part.shape[2]
    quarter = mid.shape[2]
    piece = turned.shape[2]

    def seq_peer(d):
        d = lax.rem(d - 1 + lax.rem(lane, 2) * 3, SEQ - 1) + 1
        return lax.rem(along_z + lax.div(d, 2), 4) * 2 + lax.rem(high + lax.rem(d, 2), 2)

    def lane_peer(d):
        return lax.rem(lane + d, XC)

    def at_seq(p):
        return {"seq": p, "grp": grp}

    def at_lane(p):
        return {"seq": seq, "grp": row * XC + p}

    def at_y(p):
        return {"seq": along_z * 2 + lax.div(p, 2), "grp": lax.rem(p, 2) * XC + lane}

    def at_z(p):
        return {"seq": p * 2 + high, "grp": grp}

    turn_to = {"seq": lane, "grp": row * XC + seq}
    other_row = {"seq": seq, "grp": (1 - row) * XC + lane}
    other_corner = {"seq": along_z * 2 + 1 - high, "grp": (1 - row) * XC + lane}

    def columns(owner, h):
        return pl.ds(pl.multiple_of((owner * heads + h) * HD, HD), HD)

    def part_rows(owner, size):
        return pl.ds(pl.multiple_of(owner * size, size), size)

    def token_rows(owner):
        return part_rows(owner, tokens)

    def remote(src, dst, send, recv, where):
        pltpu.make_async_remote_copy(
            src_ref=src, dst_ref=dst, send_sem=send, recv_sem=recv, device_id=where, device_id_type=MESH
        ).start()

    def local(src, dst, sem):
        pltpu.make_async_copy(src, dst, sem).start()

    def drain(ref, sem):
        pltpu.make_async_copy(ref, ref, sem).wait()

    def load_ctx(h, carry):
        local(ck.at[:, columns(lane, h)], ctx.at[0, h], ctx_sem)
        local(cv.at[:, columns(lane, h)], ctx.at[1, h], ctx_sem)
        return carry

    lax.fori_loop(0, heads, load_ctx, 0)

    barrier = pltpu.get_barrier_semaphore()

    def greet(d, carry):
        pl.semaphore_signal(barrier, inc=1, device_id=at_seq(seq_peer(d)), device_id_type=MESH)
        pl.semaphore_signal(barrier, inc=1, device_id=at_lane(lane_peer(d)), device_id_type=MESH)
        return carry

    lax.fori_loop(1, SEQ, greet, 0)
    pl.semaphore_signal(barrier, inc=1, device_id=other_row, device_id_type=MESH)
    pl.semaphore_signal(barrier, inc=1, device_id=other_corner, device_id_type=MESH)

    @pl.when(lane != seq)
    def _():
        pl.semaphore_signal(barrier, inc=1, device_id=turn_to, device_id_type=MESH)
        pl.semaphore_wait(barrier, SEQ + XC + 1)

    @pl.when(lane == seq)
    def _():
        pl.semaphore_wait(barrier, SEQ + XC)

    def send_cross(h, carry):
        for a, ref in enumerate((cq, cu)):
            local(ref.at[0, :, columns(lane, h)], cross_in.at[h, a, token_rows(lane)], x_recv.at[h])

        def to_peer(d, inner):
            e = lane_peer(d)
            for a, ref in enumerate((cq, cu)):
                remote(
                    ref.at[0, :, columns(e, h)], cross_in.at[h, a, token_rows(lane)],
                    x_send, x_recv.at[h], at_lane(e),
                )
            return inner

        lax.fori_loop(1, XC, to_peer, 0)
        return carry

    def send_self(h, carry):

        def to_peer(d, inner):
            p = seq_peer(d)
            for a, ref in enumerate((sq, sk, sv, su)):
                remote(
                    ref.at[0, :, columns(p, h)], self_in.at[h, a, token_rows(seq)],
                    in_send, in_recv.at[h], at_seq(p),
                )
            return inner

        lax.fori_loop(1, SEQ, to_peer, 0)
        for a, ref in enumerate((sq, sk, sv, su)):
            local(ref.at[0, :, columns(seq, h)], self_in.at[h, a, token_rows(seq)], in_recv.at[h])
        return carry

    def send_both(h, carry):
        send_self(h, carry)
        return send_cross(h, carry)

    lax.fori_loop(0, EARLY, send_both, 0)
    lax.fori_loop(EARLY, heads, send_cross, 0)

    drain(ctx, ctx_sem)

    def cross_head(h, carry):
        drain(cross_in.at[h], x_recv.at[h])
        key_acc[pl.ds(0, text), :] = jnp.zeros((text, HD), jnp.float32)
        value_acc[pl.ds(0, text), :] = jnp.zeros((text, HD), jnp.float32)

        def block(b, inner):
            at = pl.ds(pl.multiple_of(b * BLOCK, BLOCK), BLOCK)
            query_grad, key_grad, value_grad = attend_block(
                cross_in[h, 0, at, :], cross_in[h, 1, at, :], ctx[0, h], ctx[1, h]
            )
            cross_out[h, at, :] = query_grad.astype(jnp.bfloat16)
            key_acc[pl.ds(0, text), :] += key_grad
            value_acc[pl.ds(0, text), :] += value_grad
            return inner

        lax.fori_loop(0, rows // BLOCK, block, 0)
        part[h, 0] = (key_acc[pl.ds(0, text), :] * SCALE).astype(jnp.bfloat16)
        part[h, 1] = value_acc[pl.ds(0, text), :].astype(jnp.bfloat16)

        local(part.at[h, 0, part_rows(along_y, quarter)], first.at[0, along_y, h], a_recv)
        local(part.at[h, 1, part_rows(along_z, quarter)], first.at[1, along_z, h], a_recv)

        def to_quarter(d, inner):
            p = lax.rem(along_y + d, 4)
            remote(part.at[h, 0, part_rows(p, quarter)], first.at[0, along_y, h], a_send, a_recv, at_y(p))
            p = lax.rem(along_z + d, 4)
            remote(part.at[h, 1, part_rows(p, quarter)], first.at[1, along_z, h], a_send, a_recv, at_z(p))
            return inner

        lax.fori_loop(1, 4, to_quarter, 0)

        local(cross_out.at[h, token_rows(lane)], ocq.at[0, :, columns(lane, h)], xo_recv)

        def to_peer(d, inner):
            e = lane_peer(d)
            remote(
                cross_out.at[h, token_rows(e)], ocq.at[0, :, columns(lane, h)], xo_send, xo_recv, at_lane(e)
            )
            return inner

        lax.fori_loop(1, XC, to_peer, 0)
        return carry

    lax.fori_loop(0, heads, cross_head, 0)

    def sum_quarters():
        drain(first, a_recv)

        def one(h, carry):
            for a in range(2):
                total = first[a, 0, h].astype(jnp.float32)
                for i in range(1, 4):
                    total = total + first[a, i, h].astype(jnp.float32)
                mid[a, h] = total.astype(jnp.bfloat16)
            return carry

        lax.fori_loop(0, heads, one, 0)
        local(mid.at[0, :, part_rows(along_z, piece)], second.at[0, along_z], b_recv)
        local(mid.at[1, :, part_rows(along_y, piece)], second.at[1, along_y], b_recv)

        def to_piece(d, carry):
            p = lax.rem(along_z + d, 4)
            remote(mid.at[0, :, part_rows(p, piece)], second.at[0, along_z], b_send, b_recv, at_z(p))
            p = lax.rem(along_y + d, 4)
            remote(mid.at[1, :, part_rows(p, piece)], second.at[1, along_y], b_send, b_recv, at_y(p))
            return carry

        lax.fori_loop(1, 4, to_piece, 0)

    def sum_pieces():
        drain(second, b_recv)
        for a in range(2):
            total = second[a, 0].astype(jnp.float32)
            for i in range(1, 4):
                total = total + second[a, i].astype(jnp.float32)
            turned[a] = total.astype(jnp.bfloat16)

        @pl.when(lane == seq)
        def _():
            local(turned, gathered.at[lane, row], t_recv)

        @pl.when(lane != seq)
        def _():
            remote(turned, gathered.at[seq, row], t_send, t_recv, turn_to)

    def share_rows():
        drain(turned, t_recv)
        remote(gathered.at[lane, row], gathered.at[lane, row], y_send, y_recv, other_row)

    def share_lanes():
        drain(turned, y_recv)

        def to_lane(d, inner):
            remote(gathered.at[lane], gathered.at[lane], g_send, g_recv, at_lane(lane_peer(d)))
            return inner

        lax.fori_loop(1, XC, to_lane, 0)

    def self_head(h, carry):
        @pl.when(h == 0)
        def _():
            send_self(EARLY, 0)

        for position, step in enumerate((sum_quarters, sum_pieces, share_rows, share_lanes)):
            pl.when(h == STAGES[position])(step)

        @pl.when(h == LATE)
        def _():
            send_self(EARLY + 1, 0)

        drain(self_in.at[h], in_recv.at[h])
        key_acc[...] = jnp.zeros_like(key_acc)
        value_acc[...] = jnp.zeros_like(value_acc)

        def block(b, inner):
            at = pl.ds(pl.multiple_of(b * BLOCK, BLOCK), BLOCK)
            query_grad, key_grad, value_grad = attend_block(
                self_in[h, 0, at, :], self_in[h, 3, at, :], self_in[h, 1], self_in[h, 2]
            )
            self_out[h, 0, at, :] = query_grad.astype(jnp.bfloat16)
            key_acc[...] += key_grad
            value_acc[...] += value_grad
            return inner

        lax.fori_loop(0, rows // BLOCK, block, 0)
        self_out[h, 1] = (key_acc[...] * SCALE).astype(jnp.bfloat16)
        self_out[h, 2] = value_acc[...].astype(jnp.bfloat16)

        for a, ref in enumerate((oq, ok, ov)):
            local(self_out.at[h, a, token_rows(seq)], ref.at[0, :, columns(seq, h)], o_recv.at[a])

        def to_peer(d, inner):
            p = seq_peer(d)
            for a, ref in enumerate((oq, ok, ov)):
                remote(
                    self_out.at[h, a, token_rows(p)], ref.at[0, :, columns(seq, h)],
                    o_send, o_recv.at[a], at_seq(p),
                )
            return inner

        lax.fori_loop(1, SEQ, to_peer, 0)
        return carry

    lax.fori_loop(0, heads, self_head, 0)

    drain(gathered.at[pl.ds(0, XC - 1)], g_recv)
    for h in range(heads):
        at = pl.ds(h * HD, HD)
        for e in range(XC):
            z, y_high = divmod(e, 2)
            for r in range(2):
                y = y_high * 2 + r
                ock[pl.ds(y * quarter + z * piece, piece), at] = gathered[e, r, 0, h].astype(jnp.float32)
                ocv[pl.ds(z * quarter + y * piece, piece), at] = gathered[e, r, 1, h].astype(jnp.float32)

    others = rows - tokens
    drain(self_in.at[:, :, pl.ds(0, others)], in_send)
    drain(cross_in.at[:, :, pl.ds(0, others)], x_send)
    drain(cross_out.at[:, pl.ds(0, others)], xo_send)
    drain(first.at[:, pl.ds(0, 3)], a_send)
    drain(second.at[:, pl.ds(0, 3)], b_send)

    @pl.when(lane != seq)
    def _():
        drain(turned, t_send)

    drain(turned, y_send)
    drain(gathered.at[pl.ds(0, XC - 1)], g_send)
    drain(self_out.at[:, :, pl.ds(0, others)], o_send)
    drain(ocq, xo_recv)
    for a, ref in enumerate((oq, ok, ov)):
        drain(ref, o_recv.at[a])


def to_hbm(*refs):
    count = len(refs) // 2
    sems = refs[-1]
    copies = []
    for i in range(count):
        rows = refs[i].shape[-2] // CHUNKS
        for j in range(CHUNKS):
            at = (0,) * (len(refs[i].shape) - 2) + (pl.ds(j * rows, rows),)
            copies.append(pltpu.make_async_copy(refs[i].at[at], refs[count + i].at[at], sems.at[i, j]))
    for copy in copies:
        copy.start()
    for copy in copies:
        copy.wait()


def shards(sq, sk, sv, su, cq, ck, cv, cu):
    tokens, width = sq.shape[1], sq.shape[2]
    text = ck.shape[0]
    rows = tokens * SEQ
    heads = width // HD // SEQ
    quarter, piece = text // 4, text // 16
    half, full = jnp.bfloat16, jnp.float32
    token_shape = ((1, tokens, width), half)
    text_shape = ((text, width // SEQ), full)
    out_shapes = (token_shape,) * 4 + (text_shape,) * 2
    in_any = pl.BlockSpec(memory_space=pl.ANY)
    in_vmem = pl.BlockSpec(memory_space=pltpu.VMEM)
    dma = pltpu.SemaphoreType.DMA
    results = pl.pallas_call(
        kernel,
        out_shape=tuple(pltpu.VMEM(*shape) for shape in out_shapes),
        in_specs=[in_any] * 8,
        out_specs=(in_vmem,) * 6,
        scratch_shapes=[
            pltpu.VMEM((heads, 4, rows, HD), half),
            pltpu.VMEM((heads, 2, rows, HD), half),
            pltpu.VMEM((2, heads, text, HD), half),
            pltpu.VMEM((heads, 3, rows, HD), half),
            pltpu.VMEM((heads, rows, HD), half),
            pltpu.VMEM((heads, 2, text, HD), half),
            pltpu.VMEM((2, 4, heads, quarter, HD), half),
            pltpu.VMEM((2, heads, quarter, HD), half),
            pltpu.VMEM((2, 4, heads, piece, HD), half),
            pltpu.VMEM((2, heads, piece, HD), half),
            pltpu.VMEM((XC, 2, 2, heads, piece, HD), half),
            pltpu.VMEM((rows, HD), full),
            pltpu.VMEM((rows, HD), full),
            dma, dma((heads,)), dma, dma((heads,)), dma, dma, dma((3,)), dma, dma,
            dma, dma, dma, dma, dma, dma, dma, dma, dma, dma,
        ],
        compiler_params=pltpu.CompilerParams(
            collective_id=0, has_side_effects=True, vmem_limit_bytes=46 << 20
        ),
        cost_estimate=pl.CostEstimate(flops=10 << 30, bytes_accessed=16 << 20, transcendentals=8 << 20),
    )(sq, sk, sv, su, cq, ck, cv, cu)
    return pl.pallas_call(
        to_hbm,
        out_shape=tuple(jax.ShapeDtypeStruct(*shape) for shape in out_shapes),
        in_specs=[in_vmem] * 6,
        out_specs=(in_any,) * 6,
        scratch_shapes=[dma((6, CHUNKS))],
        compiler_params=pltpu.CompilerParams(vmem_limit_bytes=1 << 20),
    )(*results)


def solution(mesh):
    token = P("grp", "seq", None)
    return jax.shard_map(
        shards,
        mesh=mesh,
        in_specs=(token, token, token, token, token, P(), P(), token),
        out_specs=(token, token, token, token, P(None, "seq"), P(None, "seq")),
        check_vma=False,
    )
```

```python
import functools
import math

import jax
import jax.numpy as jnp
from jax import lax
from jax.experimental import pallas as pl
from jax.experimental.pallas import tpu as pltpu
from jax.sharding import PartitionSpec as P

HD = 128
SEQ = 8
XC = 8
MESH = pl.DeviceIdType.MESH
SCALE = HD ** (-0.5)
EXP2_SCALE = SCALE * math.log2(math.e)
BLOCK = 256
CHUNKS = 4
EARLY = 3
LATE = 1
STAGES = (1, 2, 3, 4)


def contract(left, right, left_dim, right_dim):
    return lax.dot_general(
        left, right, (((left_dim,), (right_dim,)), ((), ())), preferred_element_type=jnp.float32
    )


def attend_block(queries, upstream, keys, values):
    scores = contract(keys, queries, 1, 1)
    top = jnp.max(scores, axis=0, keepdims=True)
    raised = jnp.exp2((scores - top) * EXP2_SCALE)
    weights = raised * (1.0 / jnp.sum(raised, axis=0, keepdims=True))
    rounded = weights.astype(jnp.bfloat16)
    grad_prob = contract(values, upstream, 1, 1)
    delta = jnp.sum(rounded.astype(jnp.float32) * grad_prob, axis=0, keepdims=True)
    grad_score = (weights * (grad_prob - delta)).astype(jnp.bfloat16)
    value_grad = contract(rounded, upstream, 1, 0)
    key_grad = contract(grad_score, queries, 1, 0)
    query_grad = contract(keys, grad_score, 0, 0).T * SCALE
    return query_grad, key_grad, value_grad


def kernel(
    sq, sk, sv, su, cq, ck, cv, cu,
    oq, ok, ov, ocq, ock, ocv,
    self_in, cross_in, ctx, self_out, cross_out, part, first, mid, second, turned, gathered,
    key_acc, value_acc,
    in_send, in_recv, x_send, x_recv, ctx_sem, o_send, o_recv, xo_send, xo_recv,
    a_send, a_recv, b_send, b_recv, t_send, t_recv, y_send, y_recv, g_send, g_recv,
):
    seq = lax.axis_index("seq")
    grp = lax.axis_index("grp")
    lane = lax.rem(grp, XC)
    row = lax.div(grp, XC)
    along_z = lax.div(seq, 2)
    high = lax.rem(seq, 2)
    along_y = high * 2 + row
    heads = self_in.shape[0]
    tokens = sq.shape[1]
    rows = self_in.shape[2]
    text = part.shape[2]
    quarter = mid.shape[2]
    piece = turned.shape[2]

    def seq_peer(d):
        d = lax.rem(d - 1 + lax.rem(lane, 2) * 3, SEQ - 1) + 1
        return lax.rem(along_z + lax.div(d, 2), 4) * 2 + lax.rem(high + lax.rem(d, 2), 2)

    def lane_peer(d):
        return lax.rem(lane + d, XC)

    def at_seq(p):
        return {"seq": p, "grp": grp}

    def at_lane(p):
        return {"seq": seq, "grp": row * XC + p}

    def at_y(p):
        return {"seq": along_z * 2 + lax.div(p, 2), "grp": lax.rem(p, 2) * XC + lane}

    def at_z(p):
        return {"seq": p * 2 + high, "grp": grp}

    core = lax.rem(lane, 2)
    turn_to = {"seq": lane, "grp": row * XC + lax.rem(seq + lane - core, SEQ)}
    held = lax.rem(lane - seq + high + SEQ, SEQ)
    turn_from = {"seq": held, "grp": row * XC + seq}
    stays = (lane == seq) & (seq == core)
    moves = (lane != seq) | (seq != core)
    other_row = {"seq": seq, "grp": (1 - row) * XC + lane}
    other_corner = {"seq": along_z * 2 + 1 - high, "grp": (1 - row) * XC + lane}

    def columns(owner, h):
        return pl.ds(pl.multiple_of((owner * heads + h) * HD, HD), HD)

    def part_rows(owner, size):
        return pl.ds(pl.multiple_of(owner * size, size), size)

    def token_rows(owner):
        return part_rows(owner, tokens)

    def remote(src, dst, send, recv, where):
        pltpu.make_async_remote_copy(
            src_ref=src, dst_ref=dst, send_sem=send, recv_sem=recv, device_id=where, device_id_type=MESH
        ).start()

    def local(src, dst, sem):
        pltpu.make_async_copy(src, dst, sem).start()

    def drain(ref, sem):
        pltpu.make_async_copy(ref, ref, sem).wait()

    def load_ctx(h, carry):
        local(ck.at[:, columns(lane, h)], ctx.at[0, h], ctx_sem)
        local(cv.at[:, columns(lane, h)], ctx.at[1, h], ctx_sem)
        return carry

    lax.fori_loop(0, heads, load_ctx, 0)

    barrier = pltpu.get_barrier_semaphore()

    def greet(d, carry):
        pl.semaphore_signal(barrier, inc=1, device_id=at_seq(seq_peer(d)), device_id_type=MESH)
        pl.semaphore_signal(barrier, inc=1, device_id=at_lane(lane_peer(d)), device_id_type=MESH)
        return carry

    lax.fori_loop(1, SEQ, greet, 0)
    pl.semaphore_signal(barrier, inc=1, device_id=other_row, device_id_type=MESH)
    pl.semaphore_signal(barrier, inc=1, device_id=other_corner, device_id_type=MESH)

    @pl.when(moves)
    def _():
        pl.semaphore_signal(barrier, inc=1, device_id=turn_to, device_id_type=MESH)
        pl.semaphore_signal(barrier, inc=1, device_id=turn_from, device_id_type=MESH)
        pl.semaphore_wait(barrier, SEQ + XC + 2)

    @pl.when(stays)
    def _():
        pl.semaphore_wait(barrier, SEQ + XC)

    def send_cross(h, carry):
        for a, ref in enumerate((cq, cu)):
            local(ref.at[0, :, columns(lane, h)], cross_in.at[h, a, token_rows(lane)], x_recv.at[h])

        def to_peer(d, inner):
            e = lane_peer(d)
            for a, ref in enumerate((cq, cu)):
                remote(
                    ref.at[0, :, columns(e, h)], cross_in.at[h, a, token_rows(lane)],
                    x_send, x_recv.at[h], at_lane(e),
                )
            return inner

        lax.fori_loop(1, XC, to_peer, 0)
        return carry

    def send_self(h, carry):

        def to_peer(d, inner):
            p = seq_peer(d)
            for a, ref in enumerate((sq, sk, sv, su)):
                remote(
                    ref.at[0, :, columns(p, h)], self_in.at[h, a, token_rows(seq)],
                    in_send, in_recv.at[h], at_seq(p),
                )
            return inner

        lax.fori_loop(1, SEQ, to_peer, 0)
        for a, ref in enumerate((sq, sk, sv, su)):
            local(ref.at[0, :, columns(seq, h)], self_in.at[h, a, token_rows(seq)], in_recv.at[h])
        return carry

    def send_both(h, carry):
        send_self(h, carry)
        return send_cross(h, carry)

    lax.fori_loop(0, EARLY, send_both, 0)
    lax.fori_loop(EARLY, heads, send_cross, 0)

    drain(ctx, ctx_sem)

    def cross_head(h, carry):
        drain(cross_in.at[h], x_recv.at[h])
        key_acc[pl.ds(0, text), :] = jnp.zeros((text, HD), jnp.float32)
        value_acc[pl.ds(0, text), :] = jnp.zeros((text, HD), jnp.float32)

        def block(b, inner):
            at = pl.ds(pl.multiple_of(b * BLOCK, BLOCK), BLOCK)
            query_grad, key_grad, value_grad = attend_block(
                cross_in[h, 0, at, :], cross_in[h, 1, at, :], ctx[0, h], ctx[1, h]
            )
            cross_out[h, at, :] = query_grad.astype(jnp.bfloat16)
            key_acc[pl.ds(0, text), :] += key_grad
            value_acc[pl.ds(0, text), :] += value_grad
            return inner

        lax.fori_loop(0, rows // BLOCK, block, 0)
        part[h, 0] = (key_acc[pl.ds(0, text), :] * SCALE).astype(jnp.bfloat16)
        part[h, 1] = value_acc[pl.ds(0, text), :].astype(jnp.bfloat16)

        local(part.at[h, 0, part_rows(along_y, quarter)], first.at[0, along_y, h], a_recv)
        local(part.at[h, 1, part_rows(along_z, quarter)], first.at[1, along_z, h], a_recv)

        def to_quarter(d, inner):
            p = lax.rem(along_y + d, 4)
            remote(part.at[h, 0, part_rows(p, quarter)], first.at[0, along_y, h], a_send, a_recv, at_y(p))
            p = lax.rem(along_z + d, 4)
            remote(part.at[h, 1, part_rows(p, quarter)], first.at[1, along_z, h], a_send, a_recv, at_z(p))
            return inner

        lax.fori_loop(1, 4, to_quarter, 0)

        local(cross_out.at[h, token_rows(lane)], ocq.at[0, :, columns(lane, h)], xo_recv)

        def to_peer(d, inner):
            e = lane_peer(d)
            remote(
                cross_out.at[h, token_rows(e)], ocq.at[0, :, columns(lane, h)], xo_send, xo_recv, at_lane(e)
            )
            return inner

        lax.fori_loop(1, XC, to_peer, 0)
        return carry

    lax.fori_loop(0, heads, cross_head, 0)

    def sum_quarters():
        drain(first, a_recv)

        def one(h, carry):
            for a in range(2):
                total = first[a, 0, h].astype(jnp.float32)
                for i in range(1, 4):
                    total = total + first[a, i, h].astype(jnp.float32)
                mid[a, h] = total.astype(jnp.bfloat16)
            return carry

        lax.fori_loop(0, heads, one, 0)
        local(mid.at[0, :, part_rows(along_z, piece)], second.at[0, along_z], b_recv)
        local(mid.at[1, :, part_rows(along_y, piece)], second.at[1, along_y], b_recv)

        def to_piece(d, carry):
            p = lax.rem(along_z + d, 4)
            remote(mid.at[0, :, part_rows(p, piece)], second.at[0, along_z], b_send, b_recv, at_z(p))
            p = lax.rem(along_y + d, 4)
            remote(mid.at[1, :, part_rows(p, piece)], second.at[1, along_y], b_send, b_recv, at_y(p))
            return carry

        lax.fori_loop(1, 4, to_piece, 0)

    def sum_pieces():
        drain(second, b_recv)
        for a in range(2):
            total = second[a, 0].astype(jnp.float32)
            for i in range(1, 4):
                total = total + second[a, i].astype(jnp.float32)
            turned[a] = total.astype(jnp.bfloat16)

        @pl.when(stays)
        def _():
            local(turned, gathered.at[seq, row], t_recv)

        @pl.when(moves)
        def _():
            remote(turned, gathered.at[seq, row], t_send, t_recv, turn_to)

    def share_rows():
        drain(turned, t_recv)
        remote(gathered.at[held, row], gathered.at[held, row], y_send, y_recv, other_row)

    def share_lanes():
        drain(turned, y_recv)

        def to_lane(d, inner):
            remote(gathered.at[held], gathered.at[held], g_send, g_recv, at_lane(lane_peer(d)))
            return inner

        lax.fori_loop(1, XC, to_lane, 0)

    def self_head(h, carry):
        @pl.when(h == 0)
        def _():
            send_self(EARLY, 0)

        for position, step in enumerate((sum_quarters, sum_pieces, share_rows, share_lanes)):
            pl.when(h == STAGES[position])(step)

        @pl.when(h == LATE)
        def _():
            send_self(EARLY + 1, 0)

        drain(self_in.at[h], in_recv.at[h])
        key_acc[...] = jnp.zeros_like(key_acc)
        value_acc[...] = jnp.zeros_like(value_acc)

        def block(b, inner):
            at = pl.ds(pl.multiple_of(b * BLOCK, BLOCK), BLOCK)
            query_grad, key_grad, value_grad = attend_block(
                self_in[h, 0, at, :], self_in[h, 3, at, :], self_in[h, 1], self_in[h, 2]
            )
            self_out[h, 0, at, :] = query_grad.astype(jnp.bfloat16)
            key_acc[...] += key_grad
            value_acc[...] += value_grad
            return inner

        lax.fori_loop(0, rows // BLOCK, block, 0)
        self_out[h, 1] = (key_acc[...] * SCALE).astype(jnp.bfloat16)
        self_out[h, 2] = value_acc[...].astype(jnp.bfloat16)

        for a, ref in enumerate((oq, ok, ov)):
            local(self_out.at[h, a, token_rows(seq)], ref.at[0, :, columns(seq, h)], o_recv.at[a])

        def to_peer(d, inner):
            p = seq_peer(d)
            for a, ref in enumerate((oq, ok, ov)):
                remote(
                    self_out.at[h, a, token_rows(p)], ref.at[0, :, columns(seq, h)],
                    o_send, o_recv.at[a], at_seq(p),
                )
            return inner

        lax.fori_loop(1, SEQ, to_peer, 0)
        return carry

    lax.fori_loop(0, heads, self_head, 0)

    drain(gathered.at[pl.ds(0, XC - 1)], g_recv)
    for h in range(heads):
        at = pl.ds(h * HD, HD)
        for e in range(XC):
            z, y_high = divmod(e, 2)
            for r in range(2):
                y = y_high * 2 + r
                ock[pl.ds(y * quarter + z * piece, piece), at] = gathered[e, r, 0, h].astype(jnp.float32)
                ocv[pl.ds(z * quarter + y * piece, piece), at] = gathered[e, r, 1, h].astype(jnp.float32)

    others = rows - tokens
    drain(self_in.at[:, :, pl.ds(0, others)], in_send)
    drain(cross_in.at[:, :, pl.ds(0, others)], x_send)
    drain(cross_out.at[:, pl.ds(0, others)], xo_send)
    drain(first.at[:, pl.ds(0, 3)], a_send)
    drain(second.at[:, pl.ds(0, 3)], b_send)

    @pl.when(moves)
    def _():
        drain(turned, t_send)

    drain(turned, y_send)
    drain(gathered.at[pl.ds(0, XC - 1)], g_send)
    drain(self_out.at[:, :, pl.ds(0, others)], o_send)
    drain(ocq, xo_recv)
    for a, ref in enumerate((oq, ok, ov)):
        drain(ref, o_recv.at[a])


def to_hbm(*refs):
    count = len(refs) // 2
    sems = refs[-1]
    copies = []
    for i in range(count):
        rows = refs[i].shape[-2] // CHUNKS
        for j in range(CHUNKS):
            at = (0,) * (len(refs[i].shape) - 2) + (pl.ds(j * rows, rows),)
            copies.append(pltpu.make_async_copy(refs[i].at[at], refs[count + i].at[at], sems.at[i, j]))
    for copy in copies:
        copy.start()
    for copy in copies:
        copy.wait()


def shards(sq, sk, sv, su, cq, ck, cv, cu):
    tokens, width = sq.shape[1], sq.shape[2]
    text = ck.shape[0]
    rows = tokens * SEQ
    heads = width // HD // SEQ
    quarter, piece = text // 4, text // 16
    half, full = jnp.bfloat16, jnp.float32
    token_shape = ((1, tokens, width), half)
    text_shape = ((text, width // SEQ), full)
    out_shapes = (token_shape,) * 4 + (text_shape,) * 2
    in_any = pl.BlockSpec(memory_space=pl.ANY)
    in_vmem = pl.BlockSpec(memory_space=pltpu.VMEM)
    dma = pltpu.SemaphoreType.DMA
    results = pl.pallas_call(
        kernel,
        out_shape=tuple(pltpu.VMEM(*shape) for shape in out_shapes),
        in_specs=[in_any] * 8,
        out_specs=(in_vmem,) * 6,
        scratch_shapes=[
            pltpu.VMEM((heads, 4, rows, HD), half),
            pltpu.VMEM((heads, 2, rows, HD), half),
            pltpu.VMEM((2, heads, text, HD), half),
            pltpu.VMEM((heads, 3, rows, HD), half),
            pltpu.VMEM((heads, rows, HD), half),
            pltpu.VMEM((heads, 2, text, HD), half),
            pltpu.VMEM((2, 4, heads, quarter, HD), half),
            pltpu.VMEM((2, heads, quarter, HD), half),
            pltpu.VMEM((2, 4, heads, piece, HD), half),
            pltpu.VMEM((2, heads, piece, HD), half),
            pltpu.VMEM((XC, 2, 2, heads, piece, HD), half),
            pltpu.VMEM((rows, HD), full),
            pltpu.VMEM((rows, HD), full),
            dma, dma((heads,)), dma, dma((heads,)), dma, dma, dma((3,)), dma, dma,
            dma, dma, dma, dma, dma, dma, dma, dma, dma, dma,
        ],
        compiler_params=pltpu.CompilerParams(
            collective_id=0, has_side_effects=True, vmem_limit_bytes=46 << 20
        ),
        cost_estimate=pl.CostEstimate(flops=10 << 30, bytes_accessed=16 << 20, transcendentals=8 << 20),
    )(sq, sk, sv, su, cq, ck, cv, cu)
    return pl.pallas_call(
        to_hbm,
        out_shape=tuple(jax.ShapeDtypeStruct(*shape) for shape in out_shapes),
        in_specs=[in_vmem] * 6,
        out_specs=(in_any,) * 6,
        scratch_shapes=[dma((6, CHUNKS))],
        compiler_params=pltpu.CompilerParams(vmem_limit_bytes=1 << 20),
    )(*results)


def solution(mesh):
    token = P("grp", "seq", None)
    return jax.shard_map(
        shards,
        mesh=mesh,
        in_specs=(token, token, token, token, token, P(), P(), token),
        out_specs=(token, token, token, token, P(None, "seq"), P(None, "seq")),
        check_vma=False,
    )
```
